32 devices in a mesh: gx: 2 (over core), gy: 2 (over x), gz: 8 (over z, y).
Axes of the slice: x: 2, y: 2, z: 4, core: 2. Of those that a mesh axis runs over, the one named last changes fastest.
Arguments:
- zvecs: bfloat16 [64, 3, 64, 4096], P(('gx', 'gy', 'gz')), may hold values from -0.0546875 to 0.0546875
- counts: int32 [64], P(('gx', 'gy', 'gz')), may hold values from 16 to 64
- adjacency: int32 [64, 6], P(('gx', 'gy', 'gz')), may hold values from -1 to 63, as said below
- mat_id: int32 [64], replicated, may hold values from 0 to 15
- shear: float32 [16], replicated, may hold values from 0.25 to 4
- ratio: float32 [16], replicated, may hold values from 0.5 to 2
- owner_map: int32 [4, 16], P(('gx', 'gy')), may hold values from 0 to 15, each once within a row
Outputs:
- agglom: float32 [4, 16, 7, 4096], P(('gx', 'gy'), 'gz')
The draws below stay inside these ranges and needn't reach their ends.
Inputs may be any that keep to these rules, and one draw needn't show every extreme that they name: For each direction d, adjacency[i, 2 d + 1] = j names a subdomain of the next device along the d-th mesh axis (gx, gy, gz, device index (ix * 2 + iy) * 8 + iz holding subdomains index * 2 to index * 2 + 1) and then adjacency[j, 2 d] = i; -1 exactly where the device is the last (for 2 d + 1) or first (for 2 d) along that axis.
All inputs are finite; a program needn't handle non-finite values.
Results may differ from the reference program's by a relative error of at most 0.0003.
Values may be sent and summed in bfloat16 or wider, within the bound.
No kernel may reach another device: no remote copies, remote signals or barrier semaphores. Data moves between devices by JAX's collectives and lax.ppermute only.
A program may use at most 192 MiB of HBM per device.

```python
import math
import jax
import jax.numpy as jnp
from jax import lax

NV = 64
SUB_DEV = 2
BX = 16
BY = 16
BZ = 16
NMAT = 16
CELLS = 4096
SUBS = 64
COL = 16
COLUMNS = 4
N_GX = 2
N_GY = 2
N_GZ = 8


def draw_adjacency(key, part):
    grid = (N_GX, N_GY, N_GZ, SUB_DEV)
    xpos = lax.broadcasted_iota(jnp.int32, grid, 0)
    ypos = lax.broadcasted_iota(jnp.int32, grid, 1)
    zpos = lax.broadcasted_iota(jnp.int32, grid, 2)
    local = lax.broadcasted_iota(jnp.int32, grid, 3)
    device = (xpos * N_GY + ypos) * N_GZ + zpos
    columns = []
    for axis, extent, stride, where_at in ((0, N_GX, N_GY * N_GZ, xpos), (1, N_GY, N_GZ, ypos), (2, N_GZ, 1, zpos)):
        scores = jax.random.randint(jax.random.fold_in(key, 17 + axis), grid, 0, 1 << 20)
        scores = scores * SUB_DEV + local
        forward = jnp.argsort(scores, axis=3, stable=True).astype(jnp.int32)
        backward = jnp.argsort(forward, axis=3, stable=True).astype(jnp.int32)
        before = jnp.roll(backward, 1, axis=axis)
        lower = jnp.where(where_at > 0, (device - stride) * SUB_DEV + before, -1)
        upper = jnp.where(where_at < extent - 1, (device + stride) * SUB_DEV + forward, -1)
        columns.append(lower)
        columns.append(upper)
    return jnp.stack(columns, -1).reshape(N_GX * N_GY * N_GZ * SUB_DEV, 6).astype(jnp.int32)


def place_ends(values, key, low, largest):
    spot = [jax.random.randint(jax.random.fold_in(key, axis), (), 0, length) for axis, length in enumerate(values.shape)]
    widest = values.shape.index(max(values.shape))
    next_to = spot[:widest] + [(spot[widest] + 1) % values.shape[widest]] + spot[widest + 1:]
    return values.at[tuple(spot)].set(low).at[tuple(next_to)].set(largest)


def shard_levels(key, shape, cuts, smallest, largest):
    def one(axis_at, parts):
        steps = jax.random.uniform(jax.random.fold_in(jax.random.fold_in(key, 6), axis_at), (parts,), jnp.float32, smallest / len(cuts), largest / len(cuts))
        return jnp.repeat(jnp.exp(steps), shape[axis_at] // parts).reshape((-1,) + (1,) * (len(shape) - axis_at - 1))

    level = one(*cuts[0])
    for cut in cuts[1:]:
        level = level * one(*cut)
    return level


def noise(own_key, shape, spread, bound, cuts=(), held_as=jnp.bfloat16):
    entries = jax.random.normal(own_key, shape, jnp.float32) * spread
    if len(cuts) > 0:
        entries = shard_levels(own_key, shape, cuts, -0.22, 0.18) * entries
    return jnp.clip(entries, min=-bound, max=bound).astype(held_as)


def setup_inputs(seed: int = 0) -> dict:
    seeds = jax.random.split(jax.random.key(seed), 8)
    return {
        "zvecs": noise(seeds[0], (SUBS, 3, NV, CELLS), (3 * CELLS) ** -0.5, 0.0546875, ((0, 32),)),
        "counts": place_ends(jax.random.randint(seeds[1], (SUBS,), NV // 4, NV + 1), jax.random.fold_in(seeds[1], 1), NV // 4, NV).astype(jnp.int32),
        "adjacency": draw_adjacency(jax.random.fold_in(seeds[7], 71), 0),
        "mat_id": place_ends(jax.random.randint(seeds[3], (SUBS,), 0, NMAT), jax.random.fold_in(seeds[3], 1), 0, NMAT - 1).astype(jnp.int32),
        "shear": jnp.clip(jnp.exp(jax.random.uniform(seeds[4], (NMAT,), jnp.float32, math.log(0.25), math.log(4.0))), 0.25, 4.0),
        "ratio": jnp.clip(jax.random.uniform(seeds[5], (NMAT,), jnp.float32, 0.5, 2.0), 0.5, 2.0),
        "owner_map": jax.vmap(lambda own: jax.random.permutation(own, COL))(jax.random.split(seeds[6], COLUMNS)).reshape((COLUMNS, COL)).astype(jnp.int32),
    }


def stencil(u, coef):
    cell = lax.iota(jnp.int32, BX * BY * BZ)
    zpos = cell % BZ
    ypos = cell // BZ % BY
    xpos = cell // (BY * BZ)
    plain = u.astype(jnp.float32)
    total = jnp.zeros(plain.shape, jnp.float32)
    lead = [(0, 0)] * (u.ndim - 1)
    for direction, stride, where_at, extent in ((0, BY * BZ, xpos, BX), (1, BZ, ypos, BY), (2, 1, zpos, BZ)):
        upper = jnp.pad(plain[..., stride:], lead + [(0, stride)])
        upper = jnp.where(where_at < extent - 1, upper, jnp.zeros((), jnp.float32))
        lower = jnp.pad(plain[..., :-stride], lead + [(stride, 0)])
        lower = jnp.where(where_at > 0, lower, jnp.zeros((), jnp.float32))
        total = total + coef[..., direction][..., None, None] * (2.0 * plain - upper - lower)
    return total

def face(u, direction, high):
    lead = u.shape[:-1]
    block = u.reshape(lead + (BX, BY, BZ))
    if direction == 0:
        return block[..., high * (BX - 1), :, :].reshape(lead + (BY * BZ,))
    if direction == 1:
        return block[..., :, high * (BY - 1), :].reshape(lead + (BX * BZ,))
    return block[..., :, :, high * (BZ - 1)].reshape(lead + (BX * BY,))

def coefficients(ids, shear, ratio):
    onehot = (ids[..., None] == lax.iota(jnp.int32, shear.shape[0])).astype(shear.dtype)
    modulus = lax.optimization_barrier(jnp.sum(onehot * shear, -1))
    excess = lax.optimization_barrier(jnp.sum(onehot * ratio, -1))
    unit = (lax.iota(jnp.int32, 3)[:, None] == lax.iota(jnp.int32, 3)[None, :]).astype(shear.dtype)
    return modulus[..., None, None] * (1.0 + excess[..., None, None] * unit)

def reference(zvecs, counts, adjacency, mat_id, shear, ratio, owner_map):
    vector_ids = lax.iota(jnp.int32, NV)

    def masked_of(index):
        keep = vector_ids < counts[index]
        return jnp.where(keep[None, :, None], zvecs[index], jnp.zeros((), zvecs.dtype))

    def one_row(index):
        own = masked_of(index)
        own_coef = coefficients(mat_id[index], shear, ratio)
        applied = stencil(own, own_coef).astype(jnp.bfloat16)
        blocks = [jnp.einsum('cvx,cwx->vw', own.astype(jnp.float32), applied.astype(jnp.float32))]
        for slot in range(6):
            direction = slot // 2
            high = slot % 2
            other = adjacency[index, slot]
            valid = (other >= 0).astype(jnp.float32)
            safe = jnp.maximum(other, 0)
            far = masked_of(safe)
            far_coef = coefficients(mat_id[safe], shear, ratio)
            weight = -jnp.sqrt(own_coef[:, direction] * far_coef[:, direction]) * valid
            near_face = face(own, direction, high).astype(jnp.float32)
            far_face = face(far, direction, 1 - high).astype(jnp.float32)
            blocks.append(jnp.einsum('c,cvx,cwx->vw', weight, near_face, far_face))
        return jnp.stack(blocks, 0).reshape(7, NV * NV)
    rows = lax.map(one_row, jnp.arange(SUBS, dtype=jnp.int32))
    rows = rows.reshape(COLUMNS, COL, 7, NV * NV)
    inverse = jnp.argsort(owner_map, axis=1).astype(jnp.int32)
    return jnp.take_along_axis(rows, inverse[:, :, None, None], axis=1)
```

```python
import functools

import jax
import jax.numpy as jnp
from jax import lax
from jax.experimental import pallas as pl
from jax.experimental.pallas import tpu as pltpu
from jax.sharding import PartitionSpec as P

BX = 16
BY = 16
BZ = 16
PLANE = BY * BZ
LANES = 128
ALL = ("gx", "gy", "gz")
F32 = jnp.float32
BF16 = jnp.bfloat16
VMEM = pl.BlockSpec(memory_space=pltpu.VMEM)
SMEM = pl.BlockSpec(memory_space=pltpu.SMEM)
HBM = pl.BlockSpec(memory_space=pl.ANY)
DOT_T = (((1,), (1,)), ((), ()))


def lane_ids(shape):
    return lax.broadcasted_iota(jnp.int32, shape, 1)


def links_of(sizes):
    links = []
    faces = []
    for direction, axis in enumerate(("gx", "gy")):
        peers = sizes[axis]
        first = len(faces)
        if peers == 2:
            faces.append((direction, None))
            links.append((direction, None, first, first, axis, [(0, 1), (1, 0)]))
        elif peers > 2:
            up = [(i, i + 1) for i in range(peers - 1)]
            faces += [(direction, 0), (direction, 1)]
            links.append((direction, 0, first, first + 1, axis, up))
            links.append((direction, 1, first + 1, first, axis, [(j, i) for i, j in up]))
    return links, faces


def side_of(direction, side):
    if side is None:
        return 1 - lax.axis_index(ALL[direction])
    return side


def load_all(z_hbm, buf, sems):
    for i in range(buf.shape[0]):
        pltpu.make_async_copy(z_hbm.at[i], buf.at[i], sems.at[i]).start()


def faces_kernel(faces, comps, counts, z_hbm, *refs):
    out, (buf, sems) = refs[: len(faces) + 2], refs[len(faces) + 2 :]
    zlo, zhi = out[-2:]
    load_all(z_hbm, buf, sems)
    nvec = buf.shape[1]
    lane = lane_ids((nvec, LANES))
    row = lax.broadcasted_iota(jnp.int32, (nvec, LANES), 0)

    def one(i, _):
        pltpu.make_async_copy(z_hbm.at[i], buf.at[i], sems.at[i]).wait()
        keep = row < counts[i // comps]

        def put(ref, half, value):
            ref[i, :, half * LANES : (half + 1) * LANES] = jnp.where(keep, value, 0.0).astype(BF16)

        for half in range(PLANE // LANES):
            high = jnp.zeros((nvec, LANES), F32)
            low = jnp.zeros((nvec, LANES), F32)
            for x in range(BX):
                u = buf[i, :, x * PLANE + half * LANES : x * PLANE + (half + 1) * LANES].astype(F32)
                turned = pltpu.roll(u, (x - (BZ - 1)) % LANES, 1)
                high = jnp.where(lane % BZ == x, turned, high)
                low = jnp.where(lane % BZ == (x + 1) % BZ, turned, low)
            put(zhi, half, high)
            put(zlo, half, pltpu.roll(low, BZ - 1, 1))
        for ref, (direction, side) in zip(out, faces):
            h = side_of(direction, side)
            if direction == 0:
                for half in range(PLANE // LANES):
                    start = pl.multiple_of(h * ((BX - 1) * PLANE) + half * LANES, LANES)
                    put(ref, half, buf[i, :, pl.ds(start, LANES)].astype(F32))
            else:
                per = LANES // BZ
                last = (BY - 1) * BZ
                for half in range(PLANE // LANES):
                    got = jnp.zeros((nvec, LANES), F32)
                    for k in range(per):
                        x = half * per + k
                        start = pl.multiple_of(x * PLANE + h * (last // LANES * LANES), LANES)
                        u = buf[i, :, pl.ds(start, LANES)].astype(F32)
                        shift = k * BZ + h * (LANES - last % LANES)
                        turned = pltpu.roll(u, lax.rem(shift, LANES), 1)
                        got = jnp.where(lane // BZ == k, turned, got)
                    put(ref, half, got)
        return 0

    lax.fori_loop(0, buf.shape[0], one, 0)


def diagonal_kernel(subs, comps, counts, mat_id, shear, ratio, z_hbm, out, buf, mats, sems):
    load_all(z_hbm, buf, sems)
    nvec = buf.shape[1]
    device = lax.axis_index(ALL)
    i = lax.broadcasted_iota(jnp.int32, (PLANE, PLANE), 0)
    j = lax.broadcasted_iota(jnp.int32, (PLANE, PLANE), 1)
    far = jnp.abs(i - j)
    two = jnp.where(far == 0, 2.0, 0.0)
    mats[:, :PLANE] = (two - jnp.where(far == BZ, 1.0, 0.0)).astype(BF16)
    mats[:, PLANE:] = (two - jnp.where((far == 1) & (i // BZ == j // BZ), 1.0, 0.0)).astype(BF16)
    row = lax.broadcasted_iota(jnp.int32, (nvec, nvec), 0)
    col = lax.broadcasted_iota(jnp.int32, (nvec, nvec), 1)
    for s in range(subs):
        mat = mat_id[device * subs + s]
        modulus, excess = shear[mat], ratio[mat]

        def one(c, total):
            at = s * comps + c
            pltpu.make_async_copy(z_hbm.at[at], buf.at[at], sems.at[at]).wait()
            coef = [modulus * (1.0 + excess * jnp.where(c == d, 1.0, 0.0)) for d in range(3)]
            for x in range(BX):
                bits = buf[at, :, x * PLANE : (x + 1) * PLANE]
                u = bits.astype(F32)
                along = 2.0 * u
                if x < BX - 1:
                    along = along - buf[at, :, (x + 1) * PLANE : (x + 2) * PLANE].astype(F32)
                if x > 0:
                    along = along - buf[at, :, (x - 1) * PLANE : x * PLANE].astype(F32)
                inplane = jnp.dot(bits, mats[...], preferred_element_type=F32)
                applied = coef[0] * along + coef[1] * inplane[:, :PLANE] + coef[2] * inplane[:, PLANE:]
                total = total + lax.dot_general(
                    bits, applied.astype(BF16), DOT_T, preferred_element_type=F32
                )
            return total

        total = lax.fori_loop(0, comps, one, jnp.zeros((nvec, nvec), F32))
        out[s] = jnp.where((row < counts[s]) & (col < counts[s]), total, 0.0)


def couple_kernel(links, subs, comps, adjacency, mat_id, shear, ratio, *refs):
    count = len(links)
    near, far = refs[: count + 1], refs[count + 1 : 2 * count + 2]
    diagonal, out, wide = refs[2 * count + 2 :]
    nvec = diagonal.shape[1]
    device = lax.axis_index(ALL)
    blocks = count + 3
    stride = blocks * subs
    depth = nvec * nvec // LANES
    left = lane_ids((depth, LANES)) < nvec

    def coefficient(mat, c, d):
        return shear[mat] * (1.0 + ratio[mat]) if c == d else shear[mat]

    def store(places, pair):
        wide[...] = jnp.concatenate(pair, 1)
        even = wide[pl.ds(0, depth, stride=2), :]
        odd = wide[pl.ds(1, depth, stride=2), :]
        first = jnp.where(left, even, pltpu.roll(odd, nvec, 1))
        second = jnp.where(left, pltpu.roll(even, nvec, 1), odd)
        out[pl.ds(places[0], depth, stride=stride), :] = first
        out[pl.ds(places[1], depth, stride=stride), :] = second

    def weights(s, slot, direction):
        other = adjacency[s, slot]
        safe = jnp.maximum(other, 0)
        valid = jnp.where(other >= 0, 1.0, 0.0)
        own_mat, far_mat = mat_id[device * subs + s], mat_id[safe]
        values = [
            -jnp.sqrt(
                jnp.full((1, nvec), coefficient(own_mat, c, direction) * coefficient(far_mat, c, direction), F32)
            )
            * valid
            for c in range(comps)
        ]
        return lax.rem(safe, subs), values

    def product(a, at_a, b, at_b, values):
        total = None
        for c in range(comps):
            inner = lax.dot_general(
                a[at_a * comps + c], b[at_b * comps + c], DOT_T, preferred_element_type=F32
            )
            inner = inner * values[c]
            total = inner if total is None else total + inner
        return total

    store([0, 1], [diagonal[s] for s in range(subs)])
    for k, (direction, side, _, _, _, _) in enumerate(links):
        slot = 2 * direction + side_of(direction, side)
        pair = []
        for s in range(subs):
            local, values = weights(s, slot, direction)
            pair.append(product(near[k], s, far[k], local, values))
        store([(1 + k) * subs + s for s in range(subs)], pair)
    lower, upper, places = [], [], []
    for s in range(subs):
        local, values = weights(s, 4, 2)
        lower.append(product(near[count], s, far[count], local, values))
        upper.append(product(far[count], local, near[count], s, values))
        other = adjacency[s, 4]
        places.append((count + 2) * subs + jnp.where(other >= 0, lax.rem(jnp.maximum(other, 0), subs), s))
    store([(count + 1) * subs + s for s in range(subs)], lower)
    store(places, upper)


def pick_kernel(subs, blocks, owner_map, arrived, out):
    peers, rows, _ = arrived.shape
    size = rows // subs
    is_upper = lax.broadcasted_iota(jnp.int32, (size, LANES), 0) % blocks == blocks - 1

    def one(place, _):
        owner = owner_map[0, place]
        home, local = place // subs, lax.rem(place, subs)
        above = lax.rem(home + 1, peers)
        own = arrived[home, pl.ds(local, size, stride=subs), :]
        upper = arrived[above, pl.ds(local, size, stride=subs), :]
        got = jnp.where(is_upper, upper, own)
        out[owner // subs, pl.ds(lax.rem(owner, subs), size, stride=subs), :] = got
        return 0

    lax.fori_loop(0, peers * subs, one, 0)


def final_kernel(links, subs, depth, arrived, out, wide):
    count = len(links)
    blocks = count + 3
    stride = blocks * subs
    slots = out.shape[2]
    wide[...] = jnp.zeros(wide.shape, F32)
    for s in range(subs):
        for b in range(blocks):
            if b == 0:
                slot = 0
            elif b <= count:
                slot = 1 + 2 * links[b - 1][0] + side_of(*links[b - 1][:2])
            else:
                slot = 5 + b - count - 1
            block = arrived[pl.ds(b * subs + s, depth, stride=stride), :]
            wide[s, pl.ds(slot, depth, stride=8), :] = block
        for t in range(depth):
            out[0, s, :, t * LANES : (t + 1) * LANES] = wide[s, t * 8 : t * 8 + slots, :]


def per_device(sizes, zvecs, counts, adjacency, mat_id, shear, ratio, owner_map):
    subs, comps, nvec, cells = zvecs.shape
    parts = subs * comps
    peers = sizes["gz"]
    links, faces = links_of(sizes)
    flat = zvecs.reshape(parts, nvec, cells)
    depth = nvec * nvec // LANES
    blocks = len(links) + 3
    per_chunk = -(-depth // peers)
    rows = per_chunk * blocks * subs
    params = functools.partial(pltpu.CompilerParams)
    face = jax.ShapeDtypeStruct((parts, nvec, PLANE), BF16)
    got = pl.pallas_call(
        functools.partial(faces_kernel, faces, comps),
        out_shape=[face] * (len(faces) + 2),
        in_specs=[SMEM, HBM],
        out_specs=[VMEM] * (len(faces) + 2),
        scratch_shapes=[pltpu.VMEM(flat.shape, BF16), pltpu.SemaphoreType.DMA((parts,))],
        compiler_params=params(vmem_limit_bytes=24 << 20),
        name="faces",
    )(counts, flat)
    up = [(i, i + 1) for i in range(peers - 1)]
    far_z = lax.ppermute(got[-1], "gz", up)
    far = [lax.ppermute(got[sent], axis, perm) for _, _, _, sent, axis, perm in links[::-1]][::-1]
    diagonal = pl.pallas_call(
        functools.partial(diagonal_kernel, subs, comps),
        out_shape=jax.ShapeDtypeStruct((subs, nvec, nvec), F32),
        in_specs=[SMEM] * 4 + [HBM],
        out_specs=VMEM,
        scratch_shapes=[
            pltpu.VMEM(flat.shape, BF16),
            pltpu.VMEM((PLANE, 2 * PLANE), BF16),
            pltpu.SemaphoreType.DMA((parts,)),
        ],
        compiler_params=params(vmem_limit_bytes=24 << 20),
        cost_estimate=pl.CostEstimate(flops=2_000_000_000, bytes_accessed=3_200_000, transcendentals=0),
        name="diagonal",
    )(counts, mat_id, shear, ratio, flat)
    near = [got[n] for _, _, n, _, _, _ in links] + [got[-2]]
    send = pl.pallas_call(
        functools.partial(couple_kernel, links, subs, comps),
        out_shape=jax.ShapeDtypeStruct((peers * rows, LANES), F32),
        in_specs=[SMEM] * 4 + [VMEM] * (2 * len(links) + 3),
        out_specs=VMEM,
        scratch_shapes=[pltpu.VMEM((nvec, LANES), F32)],
        compiler_params=params(vmem_limit_bytes=16 << 20),
        name="couple",
    )(adjacency, mat_id, shear, ratio, *near, *far, far_z, diagonal)
    arrived = lax.all_to_all(
        send.reshape(peers, rows, LANES), "gz", split_axis=0, concat_axis=0, tiled=True
    )
    picked = pl.pallas_call(
        functools.partial(pick_kernel, subs, blocks),
        out_shape=jax.ShapeDtypeStruct((peers, rows, LANES), F32),
        in_specs=[SMEM, VMEM],
        out_specs=VMEM,
        compiler_params=params(vmem_limit_bytes=16 << 20),
        name="pick",
    )(owner_map, arrived)
    arrived = lax.all_to_all(picked, "gz", split_axis=0, concat_axis=0, tiled=True)
    return pl.pallas_call(
        functools.partial(final_kernel, links, subs, depth),
        out_shape=jax.ShapeDtypeStruct((1, subs, 7, nvec * nvec), F32),
        in_specs=[VMEM],
        out_specs=VMEM,
        scratch_shapes=[pltpu.VMEM((subs, 8 * depth, LANES), F32)],
        compiler_params=params(vmem_limit_bytes=16 << 20),
        name="final",
    )(arrived.reshape(peers * rows, LANES))


def solution(mesh):
    placed = (
        P(ALL, None, None, None),
        P(ALL),
        P(ALL, None),
        P(),
        P(),
        P(),
        P(("gx", "gy"), None),
    )
    return jax.shard_map(
        functools.partial(per_device, dict(mesh.shape)),
        mesh=mesh,
        in_specs=placed,
        out_specs=P(("gx", "gy"), "gz", None, None),
        check_vma=False,
    )
```
